256 devices in a mesh: row: 32 (over y, x, core), frame: 8 (over z).
Axes of the slice: x: 4, y: 4, z: 8, core: 2. Of those that a mesh axis runs over, the one named last changes fastest.
Arguments:
- snapshots: float32 [65536, 8192], P('row', 'frame'), may hold values from -150 to 150
- test_matrix: float32 [8192, 256], P('frame'), may hold values from -0.0625 to 0.0625
Outputs:
- basis: float32 [65536, 256], P('row')
- coefficients: float32 [256, 8192], P(None, 'frame')
The draws below stay inside these ranges and needn't reach their ends.
All inputs are finite; a program needn't handle non-finite values.
Results may differ from the reference program's by a relative error of at most 0.00014.
Values sent between devices are 32-bit elements; how exact they have to be, the bound alone decides.
A program may use at most 64 MiB of HBM per device.

```python
import math
import jax
import jax.numpy as jnp
from jax import lax

K = 256
ROWS = 65536
FRAMES = 8192


def draw_snapshots(key, part):
    key = jax.random.fold_in(key, 11)
    keys = jax.random.split(key, 3)
    row_scale = jnp.exp(jax.random.uniform(keys[0], (ROWS, 1), jnp.float32, math.log(0.3), math.log(3.0)))
    col_scale = jnp.exp(jax.random.uniform(keys[1], (1, FRAMES), jnp.float32, math.log(0.5), math.log(2.0)))
    base = jnp.clip(jax.random.normal(keys[2], (ROWS, FRAMES), jnp.float32), -5.0, 5.0)
    return base * row_scale * col_scale


def steps_of(own_key, extent, cuts, low, top_value):
    loudness = 1.0
    for position, parts in cuts:
        draws = jax.random.uniform(jax.random.fold_in(jax.random.fold_in(own_key, 6), position), (parts,), jnp.float32, low / len(cuts), top_value / len(cuts))
        loudness = loudness * jnp.repeat(jnp.exp(draws), extent[position] // parts).reshape((-1,) + (1,) * (len(extent) - 1 - position))
    return loudness


def normal_values(rng, extent, width, most, cuts=(), held_as=jnp.bfloat16):
    gain = steps_of(rng, extent, cuts, -0.22, 0.18) if cuts else 1.0
    result = jax.random.normal(rng, extent, jnp.float32) * width * gain
    return jnp.minimum(jnp.maximum(result, -most), most).astype(held_as)


def setup_inputs(seed: int = 0) -> dict:
    seeds = jax.random.split(jax.random.key(seed), 3)
    return {
        "snapshots": draw_snapshots(jax.random.fold_in(seeds[2], 71), 0),
        "test_matrix": normal_values(seeds[1], (FRAMES, K), FRAMES ** -0.5, 0.0625, ((0, 8),), jnp.float32),
    }


def reference(snapshots, test_matrix):
    highest = lax.Precision.HIGHEST
    sketch = jnp.dot(snapshots.astype(jnp.float32), test_matrix.astype(jnp.float32), precision=highest, preferred_element_type=jnp.float32)
    gram = jnp.dot(sketch.T.astype(jnp.float32), sketch.astype(jnp.float32), precision=highest, preferred_element_type=jnp.float32)
    lower = jnp.linalg.cholesky(gram)
    basis_t = jax.scipy.linalg.solve_triangular(lower, sketch.T, lower=True)
    coefficients = jnp.dot(basis_t.astype(jnp.float32), snapshots.astype(jnp.float32), precision=highest, preferred_element_type=jnp.float32)
    basis = basis_t.T * jnp.sqrt(jnp.float32(ROWS))
    return (basis, coefficients)
```

```python
import functools

import jax
import jax.numpy as jnp
from jax import lax
from jax.experimental import pallas as pl
from jax.experimental.pallas import tpu as pltpu
from jax.sharding import PartitionSpec as P

HIGHEST = lax.Precision.HIGHEST
F32 = jnp.float32
BF16 = jnp.bfloat16
MESH = pl.DeviceIdType.MESH
NF = 8
NQ = 2


def split(x):
    high = x.astype(BF16)
    return high, (x - high.astype(F32)).astype(BF16)


def mm(a, b):
    return jnp.dot(a, b, preferred_element_type=F32)


def inner(a, b):
    return lax.dot_general(a, b, (((0,), (0,)), ((), ())), precision=HIGHEST, preferred_element_type=F32)


def at(i, size):
    return pl.ds(pl.multiple_of(i * size, size), size)


def iota(shape, dim):
    return lax.broadcasted_iota(jnp.int32, shape, dim)


def panel_start(p, g, ux, tmp, m):
    word = at(lax.div(p, 2), 128)
    odd = lax.rem(p, 2)
    tmp[...] = inner(ux[:, word], ux[...])
    took = tmp[at(odd, 64), :]
    eye = jnp.where(iota((64, 256), 0) + p * 64 == iota((64, 256), 1), 1.0, 0.0)
    tmp[0:64, 0:256] = g[at(p, 64), :] - took[:, 0:256]
    tmp[0:64, 256:512] = eye - took[:, 256:512]
    block = tmp[0:64, word]
    block = jnp.where(odd == 1, pltpu.roll(block, 64, 1), block)
    row, col = iota((64, 128), 0), iota((64, 128), 1)
    m[...] = jnp.where(col < 64, block, jnp.where(col - 64 == row, 1.0, 0.0))


def eliminate(m, t):
    sub = iota((8, 128), 0)
    lanes = lambda x, k: jnp.broadcast_to(x[:, k : k + 1], (8, 128))
    subl = lambda x, k: jnp.broadcast_to(x[k : k + 1, :], (8, 128))
    tile = m[at(t, 8), :]
    others = [m[8 * i : 8 * i + 8, :] for i in range(8)]
    cols = [lanes(tile, k) for k in range(8)]
    ocols = [[lanes(o, k) for k in range(8)] for o in others]
    pivots = jnp.ones((8, 128), F32)
    for k in range(8):
        row = subl(tile, k)
        pivot = subl(cols[k], k)
        inv = 1.0 / pivot
        pivots = jnp.where(sub == k, pivot, pivots)
        mult = jnp.where(sub > k, cols[k] * inv, 0.0)
        tile = tile - mult * row
        ahead = {j: subl(cols[j], k) for j in range(k + 1, 8)}
        for j in range(k + 1, 8):
            cols[j] = cols[j] - mult * ahead[j]
        for i in range(1, 8):
            mult_i = ocols[i][k] * inv
            others[i] = others[i] - mult_i * row
            for j in range(k + 1, 8):
                ocols[i][j] = ocols[i][j] - mult_i * ahead[j]
    for i in range(8):
        rows = slice(8 * i, 8 * i + 8)
        m[rows, :] = pltpu.roll(jnp.where(i > t, others[i], m[rows, :]), 120, 1)
    m[at(t, 8), :] = pltpu.roll(tile / jnp.sqrt(pivots), 120, 1)


def panel_end(p, ux, tmp, m):
    w = jnp.where(iota((64, 64), 1) <= iota((64, 64), 0), m[:, 0:64], 0.0)
    ux[at(p, 64), :] = jnp.dot(w, tmp[0:64, :], precision=HIGHEST, preferred_element_type=F32)


def cholesky_steps(first, last, g, ux, tmp, m):
    def step(s, carry):
        p, t = lax.div(s, 8), lax.rem(s, 8)

        @pl.when(t == 0)
        def _():
            panel_start(p, g, ux, tmp, m)

        eliminate(m, t)

        @pl.when(t == 7)
        def _():
            panel_end(p, ux, tmp, m)

        return carry

    lax.fori_loop(first, last, step, 0)


def main_kernel(
    nr, a_hbm, w_hbm, s_out, x_out, c_out,
    a, a_hi, a_lo, w, w_hi, w_lo, part, rs_buf, s_full,
    g_part, g_in, g_sum, gz, g, ux, tmp, m,
    c_part, c_pair, c_half, c_in, c_all,
    a_sem, w_sem, rs_s, rs_r, ag_s, ag_r, g1_s, g1_r, gz_s, gz_r, g2_s, g2_r,
    cp_s, cp_r, c1_s, c1_r, c2_s, c2_r, cf_s, cf_r, out_sem,
):
    row, z = lax.axis_index("row"), lax.axis_index("frame")
    right, left = lax.rem(z + 1, NF), lax.rem(z + NF - 1, NF)
    core, chip = lax.rem(row, 2), lax.div(row, 2)
    mate = row + 1 - 2 * core
    nc = nr // 2
    rb = part.shape[0] // NF
    hb = rb // 2
    ahead = lambda d: lax.rem(z + d + NF, NF)
    half = lambda block, h: pl.ds(pl.multiple_of(block * rb + h * hb, hb), hb)

    def to_z(src, dst, s, r, peer):
        return pltpu.make_async_remote_copy(src, dst, s, r, device_id={"frame": peer}, device_id_type=MESH)

    def to_row(src, dst, s, r, peer):
        return pltpu.make_async_remote_copy(src, dst, s, r, device_id={"row": peer}, device_id_type=MESH)

    barrier = pltpu.get_barrier_semaphore()

    def greet_row(k, carry):
        pl.semaphore_signal(barrier, inc=1, device_id={"row": lax.rem(row + k, nr)}, device_id_type=MESH)
        return carry

    def greet_z(k, carry):
        pl.semaphore_signal(barrier, inc=1, device_id={"frame": lax.rem(z + k, NF)}, device_id_type=MESH)
        return carry

    lax.fori_loop(1, NF, greet_z, 0)
    lax.fori_loop(1, nr, greet_row, 0)

    def units(i):
        d, h = lax.div(8 - i, 2), lax.rem(i, 2)
        return half(ahead(d), h), half(ahead(-d), 1 - h)

    def load(rows, side, i):
        return pltpu.make_async_copy(a_hbm.at[rows], a.at[rows], a_sem.at[side, i])

    pltpu.make_async_copy(w_hbm, w, w_sem).start()

    def fetch(i, carry):
        for side, rows in enumerate(units(i)):
            load(rows, side, i).start()
        return carry

    lax.fori_loop(0, 8, fetch, 0)
    pltpu.make_async_copy(w_hbm, w, w_sem).wait()
    w_hi[...], w_lo[...] = split(w[...])

    def sketch(rows):
        hi, lo = split(a[rows, :])
        a_hi[rows, :], a_lo[rows, :] = hi, lo
        part[rows, :] = mm(hi, w_hi[...]) + mm(lo, w_hi[...]) + mm(hi, w_lo[...])

    def rs_copy(side, i, rows):
        return to_z(part.at[rows], rs_buf.at[side, i], rs_s.at[side, i], rs_r.at[side, i], (right, left)[side])

    def rs_step(i, carry):
        rows = units(i)
        for side in range(2):
            load(rows[side], side, i).wait()
            sketch(rows[side])

        @pl.when(i == 0)
        def _():
            pl.semaphore_wait(barrier, nr - 1 + NF - 1)

        for side in range(2):
            @pl.when(i >= 2)
            def _():
                rs_copy(side, i - 2, rows[side]).wait_recv()
                part[rows[side], :] += rs_buf[side, i - 2]

            @pl.when(i < 7)
            def _():
                rs_copy(side, i, rows[side]).start()

        return carry

    lax.fori_loop(0, 8, rs_step, 0)
    for side in range(2):
        rows = half(z, side)
        rs_copy(side, 6, rows).wait_recv()
        part[rows, :] += rs_buf[side, 6]
    own = at(z, rb)
    kc = s_full.shape[2]
    for q in range(NQ):
        s_full[q, own, :] = part[own, q * kc : (q + 1) * kc]

    def ag_copy(side, n):
        q, j = lax.div(n, 7), lax.rem(n, 7)
        e, h = lax.div(j, 2), lax.rem(j, 2)
        rows = (half(ahead(-e), h), half(ahead(e), 1 - h))[side]
        ref = s_full.at[q, rows]
        return to_z(ref, ref, ag_s.at[side, n], ag_r.at[side, n], (right, left)[side])

    def ag_send(n):
        for side in range(2):
            if n % 7 >= 2:
                ag_copy(side, n - 2).wait_recv()
            ag_copy(side, n).start()

    def ag_land(n):
        for side in range(2):
            ag_copy(side, n).wait_recv()

    ag_send(0)
    ag_send(1)

    mine = part[own, :]
    g_part[...] = inner(mine, mine)

    def g1(k):
        peer = lax.rem(row + k, nr)
        return to_row(g_part.at[at(peer, 8)], g_in.at[k], g1_s.at[k], g1_r.at[k], peer)

    def g2(k):
        piece = g.at[at(row, 8)]
        return to_row(piece, piece, g2_s.at[k], g2_r.at[k], lax.rem(row + k, nr))

    def gzc(k):
        return to_z(g_sum, gz.at[z], gz_s.at[k], gz_r.at[k], lax.rem(z + k, NF))

    def loop(first, last, f):
        def body(k, carry):
            f(k)
            return carry

        lax.fori_loop(first, last, body, 0)

    loop(1, nr, lambda k: g1(k).start())

    def project(block, q):
        rows = at(block, rb)
        hi, lo = split(s_full[q, rows, :].T)
        both = mm(jnp.concatenate([hi, lo], 0), a_hi[rows, :])
        return both[:kc] + both[kc:] + mm(hi, a_lo[rows, :])

    def add_block(d, q):
        block = ahead(d)
        if d == 0:
            c_part[q] = project(block, q)
        else:
            c_part[q] += project(block, q)

    add_block(0, 0)
    ag_send(2)
    add_block(0, 1)
    loop(1, nr, lambda k: g1(k).wait_recv())
    total = g_part[at(row, 8), :]
    for k in range(1, nr):
        total = total + g_in[k]
    g_sum[...] = total
    gz[z] = total
    loop(1, NF, lambda k: gzc(k).start())
    ag_send(3)
    add_block(-1, 0)
    add_block(1, 0)
    ag_send(4)
    loop(1, NF, lambda k: gzc(k).wait_recv())
    total = gz[0]
    for k in range(1, NF):
        total = total + gz[k]
    g[at(row, 8), :] = total
    loop(1, nr, lambda k: g2(k).start())
    ag_send(5)
    ux[...] = jnp.zeros_like(ux)
    add_block(-2, 0)
    add_block(2, 0)
    ag_send(6)
    ag_send(7)
    ag_send(8)
    loop(1, nr, lambda k: g2(k).wait_recv())

    kh = kc // 2
    wide = c_half.shape[3]

    def pair(q):
        return to_row(c_part.at[q, at(1 - core, kh)], c_pair.at[q], cp_s.at[q], cp_r.at[q], mate)

    def c1(q, k):
        peer = lax.rem(chip + k, nc)
        return to_row(c_half.at[q, peer], c_in.at[q, k], c1_s.at[q, k], c1_r.at[q, k], peer * 2 + core)

    def c2(q, k):
        piece = c_all.at[q, core, chip]
        return to_row(piece, piece, c2_s.at[q, k], c2_r.at[q, k], lax.rem(chip + k, nc) * 2 + core)

    def back(q):
        ref = c_all.at[q, core]
        return to_row(ref, ref, cf_s.at[q], cf_r.at[q], mate)

    def c_scatter(q):
        pair(q).wait_recv()
        held = c_part[q, at(core, kh), :] + c_pair[q]
        for i in range(nc):
            r, l = divmod(i, nc // (kh // 8))
            c_half[q, i] = held[8 * r : 8 * r + 8, l * wide : (l + 1) * wide]
        loop(1, nc, lambda k: c1(q, k).start())

    def c_gather(q):
        loop(1, nc, lambda k: c1(q, k).wait_recv())
        total = c_half[q, chip]
        for k in range(1, nc):
            total = total + c_in[q, k]
        c_all[q, core, chip] = total
        loop(1, nc, lambda k: c2(q, k).start())

    def c_back(q):
        loop(1, nc, lambda k: c2(q, k).wait_recv())
        back(q).start()

    chol = functools.partial(cholesky_steps, g=g, ux=ux, tmp=tmp, m=m)
    chol(0, 2)
    ag_land(5)
    add_block(-3, 0)
    add_block(3, 0)
    ag_send(9)
    ag_land(6)
    add_block(4, 0)
    pair(0).start()
    chol(2, 5)
    c_scatter(0)
    ag_send(10)
    add_block(-1, 1)
    add_block(1, 1)
    chol(5, 8)
    ag_send(11)
    chol(8, 11)
    ag_send(12)
    add_block(-2, 1)
    add_block(2, 1)
    c_gather(0)
    chol(11, 14)
    ag_send(13)
    chol(14, 20)
    c_back(0)
    ag_land(12)
    add_block(-3, 1)
    add_block(3, 1)
    ag_land(13)
    s_copy = pltpu.make_async_copy(s_full, s_out, out_sem.at[0])
    s_copy.start()
    add_block(4, 1)
    pair(1).start()
    chol(20, 23)
    c_scatter(1)
    chol(23, 28)
    c_gather(1)
    chol(28, 32)
    x_copy = pltpu.make_async_copy(ux.at[:, 256:512], x_out, out_sem.at[1])
    x_copy.start()
    c_back(1)
    for q in range(NQ):
        back(q).wait_recv()
    c_copy = pltpu.make_async_copy(c_all, c_out, out_sem.at[2])
    c_copy.start()

    def rs_done(i):
        rows = units(i)
        for side in range(2):
            rs_copy(side, i, rows[side]).wait_send()

    def ag_done(n):
        for side in range(2):
            ag_copy(side, n).wait_send()

    loop(0, 7, rs_done)
    loop(0, 7 * NQ, ag_done)
    loop(1, NF, lambda k: gzc(k).wait_send())
    loop(1, nr, lambda k: g1(k).wait_send())
    loop(1, nr, lambda k: g2(k).wait_send())
    for q in range(NQ):
        pair(q).wait_send()
        back(q).wait_send()
        loop(1, nc, lambda k: c1(q, k).wait_send())
        loop(1, nc, lambda k: c2(q, k).wait_send())
    s_copy.wait()
    x_copy.wait()
    c_copy.wait()


def main(snapshots, test_matrix, nr):
    rows, frames = snapshots.shape
    k = test_matrix.shape[1]
    rb, kc, nc = rows // NF, k // NQ, nr // 2
    wide = (kc // 2) * frames // nc // 8
    any_space = pl.BlockSpec(memory_space=pl.ANY)
    vm = lambda *shape: pltpu.VMEM(shape, F32)
    vb = lambda *shape: pltpu.VMEM(shape, BF16)
    sem = lambda *shape: pltpu.SemaphoreType.DMA(shape)
    return pl.pallas_call(
        functools.partial(main_kernel, nr),
        out_shape=(
            jax.ShapeDtypeStruct((NQ, rows, kc), F32),
            jax.ShapeDtypeStruct((k, k), F32),
            jax.ShapeDtypeStruct((NQ, 2, nc, 8, wide), F32),
        ),
        in_specs=[any_space] * 2,
        out_specs=[any_space] * 3,
        scratch_shapes=[
            vm(rows, frames), vb(rows, frames), vb(rows, frames),
            vm(frames, k), vb(frames, k), vb(frames, k),
            vm(rows, k), vm(2, 7, rb // 2, k), vm(NQ, rows, kc),
            vm(k, k), vm(nr, 8, k), vm(8, k), vm(NF, 8, k), vm(k, k),
            vm(k, 2 * k), vm(128, 2 * k), vm(64, 128),
            vm(NQ, kc, frames), vm(NQ, kc // 2, frames), vm(NQ, nc, 8, wide), vm(NQ, nc, 8, wide), vm(NQ, 2, nc, 8, wide),
            sem(2, 8), pltpu.SemaphoreType.DMA, sem(2, 7), sem(2, 7), sem(2, 7 * NQ), sem(2, 7 * NQ),
            sem(nr), sem(nr), sem(NF), sem(NF), sem(nr), sem(nr),
            sem(NQ), sem(NQ), sem(NQ, nc), sem(NQ, nc), sem(NQ, nc), sem(NQ, nc), sem(NQ), sem(NQ), sem(3),
        ],
        compiler_params=pltpu.CompilerParams(
            collective_id=0, has_side_effects=True, vmem_limit_bytes=50 * 1024 * 1024
        ),
        name="sketch_gram_projection",
    )(snapshots, test_matrix)


def finish_kernel(scale, s, x, c, basis, coef):
    x_hi, x_lo = split(x[...])
    outer = lambda a, b: lax.dot_general(a, b, (((1,), (1,)), ((), ())), preferred_element_type=F32)

    def rows_of(ref):
        return jnp.concatenate([ref[q] for q in range(NQ)], axis=1)

    hi, lo = split(rows_of(s))
    basis[...] = (outer(hi, x_hi) + outer(lo, x_hi) + outer(hi, x_lo)) * scale

    @pl.when(pl.program_id(0) == 0)
    def _():
        nq, two, nc, eight, wide = c.shape
        across = coef.shape[1] // wide
        lines = []
        for q in range(nq):
            for h in range(two):
                for r in range(nc // across):
                    lines.append(jnp.concatenate([c[q, h, r * across + l] for l in range(across)], axis=1))
        c_hi, c_lo = split(jnp.concatenate(lines, axis=0))
        coef[...] = mm(x_hi, c_hi) + mm(x_lo, c_hi) + mm(x_hi, c_lo)


def finish(s, x, c, frames, scale):
    nq, rows, kc = s.shape
    k = nq * kc
    steps = 4
    rb = rows // steps
    return pl.pallas_call(
        functools.partial(finish_kernel, scale),
        grid=(steps,),
        out_shape=(jax.ShapeDtypeStruct((rows, k), F32), jax.ShapeDtypeStruct((k, frames), F32)),
        in_specs=[
            pl.BlockSpec((nq, rb, kc), lambda i: (0, i, 0)),
            pl.BlockSpec((k, k), lambda i: (0, 0)),
            pl.BlockSpec(c.shape, lambda i: (0,) * 5),
        ],
        out_specs=[
            pl.BlockSpec((rb, k), lambda i: (i, 0)),
            pl.BlockSpec((k, frames), lambda i: (0, 0)),
        ],
        compiler_params=pltpu.CompilerParams(vmem_limit_bytes=32 * 1024 * 1024),
        name="basis_and_coefficients",
    )(s, x, c)


def on_device(nr, snapshots, test_matrix):
    s, x, c = main(snapshots, test_matrix, nr)
    scale = float((snapshots.shape[0] * nr) ** 0.5)
    return finish(s, x, c, snapshots.shape[1], scale)


def solution(mesh):
    return jax.shard_map(
        functools.partial(on_device, mesh.shape["row"]),
        mesh=mesh,
        in_specs=(P("row", "frame"), P("frame", None)),
        out_specs=(P("row", None), P(None, "frame")),
        check_vma=False,
    )
```

```python
import functools

import jax
import jax.numpy as jnp
from jax import lax
from jax.experimental import pallas as pl
from jax.experimental.pallas import tpu as pltpu
from jax.sharding import PartitionSpec as P

HIGHEST = lax.Precision.HIGHEST
F32 = jnp.float32
BF16 = jnp.bfloat16
MESH = pl.DeviceIdType.MESH
NF = 8
CHUNKS = (128, 96, 32)

PLAN = (
    ("S", 0), ("N", 0), ("R", 0, 0), ("R", 1, 0), ("R", 2, 0), ("S", 1), ("R", 0, 1), ("R", 1, 1), ("R", 2, 1),
    ("S", 2), ("S", 3), ("S", 4), ("S", 5), ("S", 6), ("R", 0, 2), ("S", 7), ("R", 1, 2), ("R", 2, 2), ("N", 1),
    ("R", 0, 3), ("R", 1, 3), ("R", 2, 3), ("N", 2), ("R", 0, 4), ("R", 1, 4), ("R", 2, 4), ("N", 3), ("R", 0, 5),
    ("R", 1, 5), ("R", 2, 5), ("N", 4), ("R", 0, 6), ("R", 1, 6), ("R", 2, 6), ("R", 0, 7), ("R", 1, 7), ("R", 2, 7),
    ("R", 0, 8), ("A", 0, 0), ("A", 0, 1), ("P", 0, 0), ("R", 1, 8), ("A", 1, 0), ("A", 1, 1), ("P", 0, 1),
    ("R", 2, 8), ("G", 0), ("P", 0, 2), ("A", 0, 2), ("A", 0, 3), ("P", -1, 0), ("P", 1, 0), ("A", 1, 2), ("A", 2, 0),
    ("A", 1, 3), ("P", -1, 1), ("P", 1, 1), ("A", 0, 4), ("G", 1), ("A", 0, 5), ("A", 2, 1), ("P", -2, 0),
    ("P", 2, 0), ("A", 1, 4), ("A", 2, 2), ("A", 0, 6), ("A", 1, 5), ("P", -2, 1), ("P", 2, 1), ("A", 0, 7),
    ("P", -3, 0), ("A", 2, 3), ("G", 2), ("P", 3, 0), ("P", -1, 2), ("A", 1, 6), ("P", 1, 2), ("A", 2, 4),
    ("A", 0, 8), ("P", 4, 0), ("C", 0, 0), ("A", 1, 7), ("P", -3, 1), ("A", 2, 5), ("P", 3, 1), ("P", -2, 2),
    ("C", 0, 1), ("P", 2, 2), ("A", 1, 8), ("P", 4, 1), ("A", 2, 6), ("C", 1, 0), ("C", 1, 1), ("G", 3), ("A", 2, 7),
    ("P", -3, 2), ("P", 3, 2), ("H", 0, 0), ("A", 2, 8), ("P", 4, 2), ("C", 2, 0), ("H", 0, 1), ("C", 2, 1),
    ("H", 1, 0), ("C", 0, 2), ("H", 1, 1), ("C", 1, 2), ("H", 2, 0), ("H", 2, 1), ("C", 2, 2), ("H", 3, 0),
    ("H", 3, 1), ("B", 0), ("C", 0, 3), ("B", 1), ("B", 2), ("B", 3), ("B", 4), ("B", 5), ("B", 6), ("D", 0),
    ("C", 1, 3), ("B", 7), ("C", 2, 3), ("D", 1), ("D", 2),
)


def split(x):
    high = x.astype(BF16)
    return high, (x - high.astype(F32)).astype(BF16)


def mm(a, b):
    return jnp.dot(a, b, preferred_element_type=F32)


def inner(a, b):
    return lax.dot_general(a, b, (((0,), (0,)), ((), ())), precision=HIGHEST, preferred_element_type=F32)


def outer(a, b, precision=None):
    return lax.dot_general(a, b, (((1,), (1,)), ((), ())), precision=precision, preferred_element_type=F32)


def at(i, size):
    return pl.ds(pl.multiple_of(i * size, size), size)


def iota(shape, dim):
    return lax.broadcasted_iota(jnp.int32, shape, dim)


def panel_begin(p, g, ux, win, m):
    lo, hi = 64 * p, 64 * p + 64
    rows = g[lo:hi, :]
    if p:
        rows = jnp.concatenate([rows[:, lo:], jnp.zeros((64, lo), F32)], axis=1)
        rows = rows - inner(ux[0:lo, lo:hi], ux[0:lo, lo : lo + 256])
    win[...] = rows
    eye = jnp.where(iota((64, 64), 0) == iota((64, 64), 1), 1.0, 0.0)
    m[...] = jnp.concatenate([rows[:, 0:64], eye], axis=1)


def eliminate(m, groups):
    sub = iota((8, 128), 0)
    lanes = lambda x, k: jnp.broadcast_to(x[:, k : k + 1], (8, 128))
    subl = lambda x, k: jnp.broadcast_to(x[k : k + 1, :], (8, 128))
    tiles = {i: m[8 * i : 8 * i + 8, :] for i in range(groups[0], 8)}
    for t in groups:
        cols = {i: [lanes(tiles[i], 8 * t + k) for k in range(8)] for i in range(t, 8)}
        pivots = jnp.ones((8, 128), F32)
        for k in range(8):
            row = subl(tiles[t], k)
            pivot = subl(cols[t][k], k)
            inv = 1.0 / pivot
            pivots = jnp.where(sub == k, pivot, pivots)
            ahead = {j: subl(cols[t][j], k) for j in range(k + 1, 8)}
            for i in range(t, 8):
                mult = cols[i][k] * inv
                if i == t:
                    mult = jnp.where(sub > k, mult, 0.0)
                tiles[i] = tiles[i] - mult * row
                for j in range(k + 1, 8):
                    cols[i][j] = cols[i][j] - mult * ahead[j]
        m[8 * t : 8 * t + 8, :] = tiles[t] / jnp.sqrt(pivots)
    for i in range(groups[-1] + 1, 8):
        m[8 * i : 8 * i + 8, :] = tiles[i]


def panel_end(p, ux, win, m):
    lo, hi = 64 * p, 64 * p + 64
    w = jnp.where(iota((64, 64), 1) <= iota((64, 64), 0), m[:, 64:128], 0.0)
    ux[lo:hi, lo : lo + 256] = jnp.dot(w, win[...], precision=HIGHEST, preferred_element_type=F32)
    ux[lo:hi, 256 + lo : 256 + hi] = w


def cholesky_step(p, half, g, ux, win, m):
    if half == 0:
        panel_begin(p, g, ux, win, m)
    eliminate(m, range(4 * half, 4 * half + 4))
    if half == 1:
        panel_end(p, ux, win, m)


def main_kernel(nr, scale, *refs):
    a_hbm, w_hbm, b_out, x_out, c_out = refs[:5]
    a, a_hi, a_lo, w, w_hi, w_lo, part, rs_buf, st = refs[5:14]
    g_part, g_in, g_sum, gz, g, ux, win, m = refs[14:22]
    c_part, c_pair, c_half, c_in, c_all = refs[22:27]
    a_sem, w_sem, rs_s, rs_r, ag_s, ag_r, g1_s, g1_r, gz_s, gz_r, g2_s, g2_r = refs[27:39]
    cp_s, cp_r, c1_s, c1_r, c2_s, c2_r, cf_s, cf_r, out_sem, near = refs[39:]
    row, z = lax.axis_index("row"), lax.axis_index("frame")
    right, left = lax.rem(z + 1, NF), lax.rem(z + NF - 1, NF)
    core, chip = lax.rem(row, 2), lax.div(row, 2)
    mate = row + 1 - 2 * core
    nc = nr // 2
    hb = st.shape[2]
    frames = a.shape[1]
    across = frames // 128
    ahead = lambda d: lax.rem(z + d + NF, NF)
    rows_of = lambda u: at(u, hb)
    starts = [sum(CHUNKS[:c]) for c in range(len(CHUNKS))]
    span = [slice(starts[c], starts[c] + CHUNKS[c]) for c in range(len(CHUNKS))]
    cut = lambda c: pl.ds(starts[c], CHUNKS[c])
    tiles = [n * across // 16 // nc for n in CHUNKS]
    slots = [pl.ds(sum(tiles[:c]), tiles[c]) for c in range(len(CHUNKS))]

    def to_z(src, dst, s, r, peer):
        return pltpu.make_async_remote_copy(src, dst, s, r, device_id={"frame": peer}, device_id_type=MESH)

    def to_row(src, dst, s, r, peer):
        return pltpu.make_async_remote_copy(src, dst, s, r, device_id={"row": peer}, device_id_type=MESH)

    def loop(first, last, f):
        def body(k, carry):
            f(k)
            return carry

        lax.fori_loop(first, last, body, 0)

    barrier = pltpu.get_barrier_semaphore()
    nx = 4
    x, y, ny = lax.rem(chip, nx), lax.div(chip, nx), nc // nx
    at_chip = lambda yy, xx: {"row": (lax.rem(yy + ny, ny) * nx + lax.rem(xx + nx, nx)) * 2 + core}
    neighbours = ({"frame": right}, {"frame": left}, {"row": mate})
    neighbours += (at_chip(y, x + 1), at_chip(y, x - 1), at_chip(y + 1, x), at_chip(y - 1, x))

    def greet(which):
        for peer in neighbours:
            pl.semaphore_signal(which, inc=1, device_id=peer, device_id_type=MESH)

    def greeted(which):
        pl.semaphore_wait(which, len(neighbours))

    def meet(stage):
        if stage:
            greeted(near.at[stage - 1])
        else:
            greeted(barrier)
        if stage < 4:
            greet(near.at[stage])

    greet(barrier)

    def units(i):
        if isinstance(i, int):
            d, h = ((8 - i) // 2, i % 2) if i < 8 else (0, 0)
        else:
            d, h = lax.div(8 - i, 2), lax.rem(i, 2)
        return 2 * ahead(d) + h, 2 * ahead(-d) + 1 - h

    def load(u, side, i):
        return pltpu.make_async_copy(a_hbm.at[rows_of(u)], a.at[rows_of(u)], a_sem.at[side, i])

    w_copy = pltpu.make_async_copy(w_hbm, w, w_sem)

    def fetch(i):
        for side, u in enumerate(units(i)):
            load(u, side, i).start()

    w_copy.start()
    fetch(0)
    fetch(1)
    ux[:, 256:512] = jnp.zeros((ux.shape[0], 256), F32)
    w_copy.wait()
    fetch(2)
    w_hi[...], w_lo[...] = split(w[...])

    def sketch(i):
        if i + 3 < 8:
            fetch(i + 3)
        for side, u in enumerate(units(i)):
            load(u, side, i).wait()
            hi, lo = split(a[rows_of(u), :])
            a_hi[rows_of(u), :], a_lo[rows_of(u), :] = hi, lo
            part[u] = (mm(hi, w_hi[...]) + mm(lo, w_hi[...]) + mm(hi, w_lo[...])).T

    def rs_copy(side, c, i, u):
        dst = rs_buf.at[side, i, cut(c)]
        return to_z(part.at[u, cut(c)], dst, rs_s.at[side], rs_r.at[side, c, i], (right, left)[side])

    def reduce_step(c, i):
        for side, u in enumerate(units(i)):
            if i >= 2:
                rs_copy(side, c, i - 2, u).wait_recv()
                total = part[u, span[c]] + rs_buf[side, i - 2, span[c]]
                if i < 8:
                    part[u, span[c]] = total
                else:
                    st[u, span[c]] = total
            if i < 7:
                rs_copy(side, c, i, u).start()

    def ag_copy(side, c, j):
        e, h = (j // 2, j % 2) if isinstance(j, int) else (lax.div(j, 2), lax.rem(j, 2))
        u = (2 * ahead(-e) + h, 2 * ahead(e) + 1 - h)[side]
        ref = st.at[u, cut(c)]
        return to_z(ref, ref, ag_s.at[side], ag_r.at[side, c, j], (right, left)[side])

    def gather_step(c, j):
        for side in range(2):
            if j >= 2:
                ag_copy(side, c, j - 2).wait_recv()
            if j < 7:
                ag_copy(side, c, j).start()

    def g1(k):
        peer = lax.rem(row + k, nr)
        return to_row(g_part.at[at(peer, 8)], g_in.at[k], g1_s, g1_r, peer)

    def g2(k):
        piece = g.at[at(row, 8)]
        return to_row(piece, piece, g2_s, g2_r, lax.rem(row + k, nr))

    def gzc(k):
        return to_z(g_sum, gz.at[z], gz_s, gz_r, lax.rem(z + k, NF))

    def g1_all():
        ref = g_in.at[pl.ds(1, nr - 1)]
        return to_row(ref, ref, g1_s, g1_r, mate)

    def gz_all():
        ref = gz.at[pl.ds(1, NF - 1)]
        return to_z(ref, ref, gz_s, gz_r, right)

    def g2_all():
        ref = g.at[pl.ds(8, 8 * (nr - 1))]
        return to_row(ref, ref, g2_s, g2_r, mate)

    def c1_all(c):
        ref = c_in.at[pl.ds(1, nc - 1), slots[c]]
        return to_row(ref, ref, c1_s.at[c], c1_r.at[c], mate)

    def c2_all(c):
        ref = c_all.at[core, pl.ds(1, nc - 1), slots[c]]
        return to_row(ref, ref, c2_s.at[c], c2_r.at[c], mate)

    def gram_step(stage):
        if stage == 0:
            mine = jnp.concatenate([st[2 * z], st[2 * z + 1]], axis=1)
            g_part[...] = outer(mine, mine, HIGHEST)
            loop(1, nr, lambda k: g1(k).start())
        elif stage == 1:
            g1_all().wait_recv()
            total = g_part[at(row, 8), :]
            for k in range(1, nr):
                total = total + g_in[k]
            g_sum[...] = total
            gz[z] = total
            loop(1, NF, lambda k: gzc(k).start())
        elif stage == 2:
            gz_all().wait_recv()
            total = gz[0]
            for k in range(1, NF):
                total = total + gz[k]
            g[at(row, 8), :] = total
            loop(1, nr, lambda k: g2(k).start())
        else:
            g2_all().wait_recv()

    def project(d, c):
        block = ahead(d)
        kc = CHUNKS[c]
        rows = at(block, 2 * hb)
        hi, lo = split(jnp.concatenate([st[2 * block, span[c]], st[2 * block + 1, span[c]]], axis=1))
        both = mm(jnp.concatenate([hi, lo], 0), a_hi[rows, :])
        total = both[:kc] + both[kc:] + mm(hi, a_lo[rows, :])
        c_part[span[c], :] = total if d == 0 else c_part[span[c], :] + total

    def pair(c):
        kh = CHUNKS[c] // 2
        src = c_part.at[pl.ds(pl.multiple_of(starts[c] + (1 - core) * kh, 8), kh)]
        return to_row(src, c_pair.at[pl.ds(starts[c] // 2, kh)], cp_s.at[c], cp_r.at[c], mate)

    def c1(c, k):
        peer = lax.rem(chip + k, nc)
        return to_row(c_half.at[peer, slots[c]], c_in.at[k, slots[c]], c1_s.at[c], c1_r.at[c], peer * 2 + core)

    def c2(c, k):
        piece = c_all.at[core, chip, slots[c]]
        return to_row(piece, piece, c2_s.at[c], c2_r.at[c], lax.rem(chip + k, nc) * 2 + core)

    def back(c):
        ref = c_all.at[core, :, slots[c]]
        return to_row(ref, ref, cf_s.at[c], cf_r.at[c], mate)

    def plane_step(c, stage):
        kh = CHUNKS[c] // 2
        if stage == 0:
            pair(c).start()
        elif stage == 1:
            pair(c).wait_recv()
            mine = pl.ds(pl.multiple_of(starts[c] + core * kh, 8), kh)
            held = c_part[mine, :] + c_pair[starts[c] // 2 : starts[c] // 2 + kh]
            for t in range(kh // 8 * across):
                r, l = divmod(t, across)
                i, s = divmod(t, tiles[c])
                c_half[i, sum(tiles[:c]) + s] = held[8 * r : 8 * r + 8, 128 * l : 128 * l + 128]
            loop(1, nc, lambda k: c1(c, k).start())
        elif stage == 2:
            c1_all(c).wait_recv()
            total = c_half[chip, slots[c]]
            for k in range(1, nc):
                total = total + c_in[k, slots[c]]
            c_all[core, chip, slots[c]] = total
            loop(1, nc, lambda k: c2(c, k).start())
        else:
            c2_all(c).wait_recv()
            back(c).start()

    def c_copy(c, h):
        piece = (h, slice(None), slots[c])
        return pltpu.make_async_copy(c_all.at[piece], c_out.at[piece], out_sem.at[c])

    def c_land(c):
        back(c).wait_recv()
        for h in range(2):
            c_copy(c, h).start()

    x_copy = pltpu.make_async_copy(ux.at[:, 256:512], x_out, out_sem.at[len(CHUNKS)])
    held_x = []

    def b_copy(i):
        rows = pl.ds(2 * hb * i, 2 * hb)
        return pltpu.make_async_copy(a.at[rows, pl.ds(0, ux.shape[0])], b_out.at[rows], out_sem.at[len(CHUNKS) + 1 + i])

    def basis_step(i):
        if i == 0:
            x_copy.start()
            held_x.extend(split(ux[:, 256:512]))
        hi, lo = split(jnp.concatenate([st[2 * i].T, st[2 * i + 1].T], axis=0))
        block = outer(hi, held_x[0]) + outer(lo, held_x[0]) + outer(hi, held_x[1])
        a[2 * hb * i : 2 * hb * (i + 1), 0 : ux.shape[0]] = block * scale
        b_copy(i).start()

    steps = {
        "N": meet,
        "S": sketch,
        "R": reduce_step,
        "A": gather_step,
        "G": gram_step,
        "P": project,
        "C": plane_step,
        "D": c_land,
        "H": functools.partial(cholesky_step, g=g, ux=ux, win=win, m=m),
        "B": basis_step,
    }
    for name, *numbers in PLAN:
        steps[name](*numbers)

    for c in range(len(CHUNKS)):
        pair(c).wait_send()
        back(c).wait_send()
        c1_all(c).wait_send()
        c2_all(c).wait_send()
    for side in range(2):
        ref = rs_buf.at[side]
        to_z(ref, ref, rs_s.at[side], rs_r.at[side, 0, 0], right).wait_send()
        to_z(ref, ref, ag_s.at[side], ag_r.at[side, 0, 0], right).wait_send()
    gz_all().wait_send()
    g1_all().wait_send()
    g2_all().wait_send()
    x_copy.wait()
    for i in range(NF):
        b_copy(i).wait()
    for c in range(len(CHUNKS)):
        for h in range(2):
            c_copy(c, h).wait()


def main(snapshots, test_matrix, nr, scale):
    rows, frames = snapshots.shape
    k = test_matrix.shape[1]
    hb, nc, nq = rows // NF // 2, nr // 2, len(CHUNKS)
    tiles = k * (frames // 128) // 16 // nc
    hbm = pl.BlockSpec(memory_space=pltpu.HBM)
    vm = lambda *shape: pltpu.VMEM(shape, F32)
    vb = lambda *shape: pltpu.VMEM(shape, BF16)
    sem = lambda *shape: pltpu.SemaphoreType.DMA(shape)
    one = pltpu.SemaphoreType.DMA
    return pl.pallas_call(
        functools.partial(main_kernel, nr, scale),
        out_shape=(
            jax.ShapeDtypeStruct((rows, k), F32),
            jax.ShapeDtypeStruct((k, k), F32),
            jax.ShapeDtypeStruct((2, nc, tiles, 8, 128), F32),
        ),
        in_specs=[hbm] * 2,
        out_specs=[hbm] * 3,
        scratch_shapes=[
            vm(rows, frames), vb(rows, frames), vb(rows, frames),
            vm(frames, k), vb(frames, k), vb(frames, k),
            vm(2 * NF, k, hb), vm(2, 7, k, hb), vm(2 * NF, k, hb),
            vm(k, k), vm(nr, 8, k), vm(8, k), vm(NF, 8, k), vm(k, k),
            vm(k, 2 * k), vm(64, k), vm(64, 128),
            vm(k, frames), vm(k // 2, frames), vm(nc, tiles, 8, 128), vm(nc, tiles, 8, 128), vm(2, nc, tiles, 8, 128),
            sem(2, 8), one, sem(2), sem(2, nq, 7), sem(2), sem(2, nq, 7),
            one, one, one, one, one, one,
            sem(nq), sem(nq), sem(nq), sem(nq), sem(nq), sem(nq), sem(nq), sem(nq), sem(nq + 1 + NF),
            pltpu.SemaphoreType.REGULAR((4,)),
        ],
        compiler_params=pltpu.CompilerParams(
            collective_id=0, has_side_effects=True, vmem_limit_bytes=62 * 1024 * 1024
        ),
        name="sketch_gram_projection",
    )(snapshots, test_matrix)


def finish_kernel(b_hbm, x_hbm, c_hbm, basis_hbm, coef_hbm, b, x, c, coef, b_sem, s_sem, in_sem, f_sem):
    parts = b_sem.shape[0]
    per = b_hbm.shape[0] // parts
    loads = [pltpu.make_async_copy(x_hbm, x, in_sem.at[0]), pltpu.make_async_copy(c_hbm, c, in_sem.at[1])]
    passed, stores = [], []
    for i in range(parts):
        rows = pl.ds(i * per, per)
        passed.append(pltpu.make_async_copy(b_hbm.at[rows], b.at[rows], b_sem.at[i]))
        stores.append(pltpu.make_async_copy(b.at[rows], basis_hbm.at[rows], s_sem.at[i]))
    for copy in loads + passed:
        copy.start()
    for load, store in zip(passed, stores):
        load.wait()
        store.start()
    loads[0].wait()
    x_hi, x_lo = split(x[...])
    loads[-1].wait()
    _, nc, total, _, _ = c.shape
    across = coef.shape[1] // 128
    lines = [None] * (x.shape[0] // 8)
    for h in range(2):
        for q, n in enumerate(CHUNKS):
            first, tiles = sum(CHUNKS[:q]) * total // x.shape[0], n * total // x.shape[0]
            for r in range(n // 16):
                line = [divmod(r * across + l, tiles) for l in range(across)]
                place = (sum(CHUNKS[:q]) + h * n // 2) // 8 + r
                lines[place] = jnp.concatenate([c[h, i, first + t] for i, t in line], axis=1)
    c_hi, c_lo = split(jnp.concatenate(lines, axis=0))
    coef[...] = mm(x_hi, c_hi) + mm(x_lo, c_hi) + mm(x_hi, c_lo)
    stores.append(pltpu.make_async_copy(coef, coef_hbm, f_sem))
    stores[-1].start()
    for copy in stores:
        copy.wait()


def finish(b, x, c, frames):
    hbm = pl.BlockSpec(memory_space=pltpu.HBM)
    vm = lambda *shape: pltpu.VMEM(shape, F32)
    return pl.pallas_call(
        finish_kernel,
        out_shape=(jax.ShapeDtypeStruct(b.shape, F32), jax.ShapeDtypeStruct((x.shape[0], frames), F32)),
        in_specs=[hbm] * 3,
        out_specs=[hbm] * 2,
        scratch_shapes=[
            vm(*b.shape), vm(*x.shape), vm(*c.shape), vm(x.shape[0], frames),
            pltpu.SemaphoreType.DMA((4,)), pltpu.SemaphoreType.DMA((4,)), pltpu.SemaphoreType.DMA((2,)), pltpu.SemaphoreType.DMA,
        ],
        compiler_params=pltpu.CompilerParams(vmem_limit_bytes=62 * 1024 * 1024),
        name="coefficients",
    )(b, x, c)


def on_device(nr, snapshots, test_matrix):
    scale = float((snapshots.shape[0] * nr) ** 0.5)
    b, x, c = main(snapshots, test_matrix, nr, scale)
    return finish(b, x, c, snapshots.shape[1])


def solution(mesh):
    return jax.shard_map(
        functools.partial(on_device, mesh.shape["row"]),
        mesh=mesh,
        in_specs=(P("row", "frame"), P("frame", None)),
        out_specs=(P("row", None), P(None, "frame")),
        check_vma=False,
    )
```

```python
import functools

import jax
import jax.numpy as jnp
from jax import lax
from jax.experimental import pallas as pl
from jax.experimental.pallas import tpu as pltpu
from jax.sharding import PartitionSpec as P

HIGHEST = lax.Precision.HIGHEST
F32 = jnp.float32
BF16 = jnp.bfloat16
MESH = pl.DeviceIdType.MESH
NF = 8
CHUNKS = (128, 128)

PLAN = (
    ("S", 0), ("N", 0), ("R", 0, 0), ("R", 1, 0), ("S", 1), ("R", 0, 1), ("R", 1, 1), ("S", 2), ("S", 3), ("S", 4),
    ("S", 5), ("R", 0, 2), ("S", 6), ("R", 1, 2), ("N", 1), ("S", 7), ("R", 0, 3), ("R", 1, 3), ("N", 2), ("R", 0, 4),
    ("R", 1, 4), ("N", 3), ("R", 0, 5), ("R", 1, 5), ("N", 4), ("R", 0, 6), ("R", 1, 6), ("R", 0, 7), ("R", 1, 7),
    ("R", 0, 8), ("A", 0, 0), ("A", 0, 1), ("P", 0, 0), ("R", 1, 8), ("A", 1, 0), ("G", 0), ("P", 0, 1), ("T", 0),
    ("A", 0, 2), ("A", 1, 1), ("A", 0, 3), ("P", -1, 0), ("P", 1, 0), ("A", 1, 2), ("A", 0, 4), ("G", 1), ("A", 1, 3),
    ("P", -1, 1), ("P", 1, 1), ("T", -1), ("T", 1), ("A", 0, 5), ("P", -2, 0), ("P", 2, 0), ("A", 1, 4), ("A", 0, 6),
    ("G", 2), ("A", 1, 5), ("P", -2, 1), ("P", 2, 1), ("T", -2), ("T", 2), ("A", 0, 7), ("P", -3, 0), ("P", 3, 0),
    ("A", 1, 6), ("A", 0, 8), ("P", 4, 0), ("C", 0, 0), ("A", 1, 7), ("P", -3, 1), ("P", 3, 1), ("C", 0, 1), ("G", 3),
    ("T", -3), ("T", 3), ("A", 1, 8), ("P", 4, 1), ("C", 1, 0), ("T", 4), ("H", 0, 0), ("H", 0, 1), ("C", 1, 1),
    ("H", 0, 2), ("H", 0, 3), ("H", 1, 0), ("H", 1, 1), ("H", 1, 2), ("H", 1, 3), ("C", 0, 2), ("H", 2, 0),
    ("H", 2, 1), ("H", 2, 2), ("H", 2, 3), ("C", 1, 2), ("H", 3, 0), ("H", 3, 1), ("H", 3, 2), ("H", 3, 3), ("B", 0),
    ("B", 1), ("B", 2), ("B", 3), ("B", 4), ("C", 0, 3), ("B", 5), ("B", 6), ("B", 7), ("D", 0), ("C", 1, 3),
    ("D", 1),
)


def split(x):
    high = x.astype(BF16)
    return high, (x - high.astype(F32)).astype(BF16)


def mm(a, b):
    return jnp.dot(a, b, preferred_element_type=F32)


def inner(a, b):
    return lax.dot_general(a, b, (((0,), (0,)), ((), ())), precision=HIGHEST, preferred_element_type=F32)


def outer(a, b, precision=None):
    return lax.dot_general(a, b, (((1,), (1,)), ((), ())), precision=precision, preferred_element_type=F32)


def at(i, size):
    return pl.ds(pl.multiple_of(i * size, size), size)


def iota(shape, dim):
    return lax.broadcasted_iota(jnp.int32, shape, dim)


def panel_begin(p, g, ux, win, m):
    lo, hi = 64 * p, 64 * p + 64
    rows = g[lo:hi, :]
    if p:
        rows = jnp.concatenate([rows[:, lo:], jnp.zeros((64, lo), F32)], axis=1)
        rows = rows - inner(ux[0:lo, lo:hi], ux[0:lo, lo : lo + 256])
    win[...] = rows
    eye = jnp.where(iota((64, 64), 0) == iota((64, 64), 1), 1.0, 0.0)
    m[...] = jnp.concatenate([rows[:, 0:64], eye], axis=1)


def eliminate(m, groups):
    sub = iota((8, 128), 0)
    lanes = lambda x, k: jnp.broadcast_to(x[:, k : k + 1], (8, 128))
    subl = lambda x, k: jnp.broadcast_to(x[k : k + 1, :], (8, 128))
    tiles = {i: m[8 * i : 8 * i + 8, :] for i in range(groups[0], 8)}
    for t in groups:
        cols = {i: [lanes(tiles[i], 8 * t + k) for k in range(8)] for i in range(t, 8)}
        pivots = jnp.ones((8, 128), F32)
        for k in range(8):
            row = subl(tiles[t], k)
            pivot = subl(cols[t][k], k)
            inv = 1.0 / pivot
            pivots = jnp.where(sub == k, pivot, pivots)
            ahead = {j: subl(cols[t][j], k) for j in range(k + 1, 8)}
            for i in range(t, 8):
                mult = cols[i][k] * inv
                if i == t:
                    mult = jnp.where(sub > k, mult, 0.0)
                tiles[i] = tiles[i] - mult * row
                for j in range(k + 1, 8):
                    cols[i][j] = cols[i][j] - mult * ahead[j]
        m[8 * t : 8 * t + 8, :] = tiles[t] / jnp.sqrt(pivots)
    for i in range(groups[-1] + 1, 8):
        m[8 * i : 8 * i + 8, :] = tiles[i]


def panel_end(p, ux, win, m):
    lo, hi = 64 * p, 64 * p + 64
    w = jnp.where(iota((64, 64), 1) <= iota((64, 64), 0), m[:, 64:128], 0.0)
    ux[lo:hi, lo : lo + 256] = jnp.dot(w, win[...], precision=HIGHEST, preferred_element_type=F32)
    ux[lo:hi, 256 + lo : 256 + hi] = w


def cholesky_step(p, quarter, g, ux, win, m):
    if quarter == 0:
        panel_begin(p, g, ux, win, m)
    eliminate(m, range(2 * quarter, 2 * quarter + 2))
    if quarter == 3:
        panel_end(p, ux, win, m)


def main_kernel(nr, scale, *refs):
    a_hbm, w_hbm, b_out, x_out, c_out = refs[:5]
    a, a_hi, a_lo, w, w_hi, w_lo, part, rs_buf, st = refs[5:14]
    g_part, g_in, g_sum, gz, g, ux, win, m = refs[14:22]
    c_part, c_pair, c_half, c_in, c_all, s_hi, s_lo = refs[22:29]
    a_sem, w_sem, rs_s, rs_r, ag_s, ag_r, g1_s, g1_r, gz_s, gz_r, g2_s, g2_r = refs[29:41]
    cp_s, cp_r, c1_s, c1_r, c2_s, c2_r, cf_s, cf_r, out_sem, near = refs[41:]
    row, z = lax.axis_index("row"), lax.axis_index("frame")
    right, left = lax.rem(z + 1, NF), lax.rem(z + NF - 1, NF)
    core, chip = lax.rem(row, 2), lax.div(row, 2)
    mate = row + 1 - 2 * core
    nc = nr // 2
    hb = st.shape[2]
    frames = a.shape[1]
    across = frames // 128
    ahead = lambda d: lax.rem(z + d + NF, NF)
    rows_of = lambda u: at(u, hb)
    starts = [sum(CHUNKS[:c]) for c in range(len(CHUNKS))]
    span = [slice(starts[c], starts[c] + CHUNKS[c]) for c in range(len(CHUNKS))]
    cut = lambda c: pl.ds(starts[c], CHUNKS[c])
    tiles = [n * across // 16 // nc for n in CHUNKS]
    slots = [pl.ds(sum(tiles[:c]), tiles[c]) for c in range(len(CHUNKS))]

    def to_z(src, dst, s, r, peer):
        return pltpu.make_async_remote_copy(src, dst, s, r, device_id={"frame": peer}, device_id_type=MESH)

    def to_row(src, dst, s, r, peer):
        return pltpu.make_async_remote_copy(src, dst, s, r, device_id={"row": peer}, device_id_type=MESH)

    def loop(first, last, f):
        def body(k, carry):
            f(k)
            return carry

        lax.fori_loop(first, last, body, 0)

    barrier = pltpu.get_barrier_semaphore()
    nx = 4
    x, y, ny = lax.rem(chip, nx), lax.div(chip, nx), nc // nx
    at_chip = lambda yy, xx: {"row": (lax.rem(yy + ny, ny) * nx + lax.rem(xx + nx, nx)) * 2 + core}
    neighbours = ({"frame": right}, {"frame": left}, {"row": mate})
    neighbours += (at_chip(y, x + 1), at_chip(y, x - 1), at_chip(y + 1, x), at_chip(y - 1, x))

    far = lambda o: min(o[0], ny - o[0]) + min(o[1], nx - o[1])
    steps_to = sorted(((dy, dx) for dy in range(ny) for dx in range(nx)), key=lambda o: (-far(o), o))
    chip_at = lambda o: lax.rem(y + o[0], ny) * nx + lax.rem(x + o[1], nx)
    both_cores = [(o, flip) for o in steps_to for flip in (0, 1)][:-2] + [((0, 0), 1)]

    def plane_peer(k):
        o, flip = both_cores[k - 1]
        return 2 * chip_at(o) + (1 - core if flip else core)

    def greet(which):
        for peer in neighbours:
            pl.semaphore_signal(which, inc=1, device_id=peer, device_id_type=MESH)

    def greeted(which):
        pl.semaphore_wait(which, len(neighbours))

    def meet(stage):
        if stage:
            greeted(near.at[stage - 1])
        else:
            greeted(barrier)
        if stage < 4:
            greet(near.at[stage])

    greet(barrier)

    def units(i):
        if isinstance(i, int):
            d, h = ((8 - i) // 2, i % 2) if i < 8 else (0, 0)
        else:
            d, h = lax.div(8 - i, 2), lax.rem(i, 2)
        return 2 * ahead(d) + h, 2 * ahead(-d) + 1 - h

    def load(u, side, i):
        return pltpu.make_async_copy(a_hbm.at[rows_of(u)], a.at[rows_of(u)], a_sem.at[side, i])

    w_copy = pltpu.make_async_copy(w_hbm, w, w_sem)

    def fetch(i):
        for side, u in enumerate(units(i)):
            load(u, side, i).start()

    w_copy.start()
    fetch(0)
    fetch(1)
    ux[:, 256:512] = jnp.zeros((ux.shape[0], 256), F32)
    w_copy.wait()
    fetch(2)
    w_hi[...], w_lo[...] = split(w[...])

    def sketch(i):
        if i + 3 < 8:
            fetch(i + 3)
        both = units(i)
        for side, u in enumerate(both):
            load(u, side, i).wait()
        hi, lo = split(jnp.concatenate([a[rows_of(u), :] for u in both], axis=0))
        for side, u in enumerate(both):
            held = slice(side * hb, (side + 1) * hb)
            a_hi[rows_of(u), :], a_lo[rows_of(u), :] = hi[held], lo[held]
        halves = mm(jnp.concatenate([hi, lo], axis=0), w_hi[...])
        total = halves[: 2 * hb] + halves[2 * hb :] + mm(hi, w_lo[...])
        for side, u in enumerate(both):
            part[u] = total[side * hb : (side + 1) * hb].T

    def rs_copy(side, c, i, u):
        dst = rs_buf.at[side, i, cut(c)]
        return to_z(part.at[u, cut(c)], dst, rs_s.at[side], rs_r.at[side, c, i], (right, left)[side])

    def reduce_step(c, i):
        for side, u in enumerate(units(i)):
            if i >= 2:
                rs_copy(side, c, i - 2, u).wait_recv()
                total = part[u, span[c]] + rs_buf[side, i - 2, span[c]]
                if i < 8:
                    part[u, span[c]] = total
                else:
                    st[u, span[c]] = total
            if i < 7:
                rs_copy(side, c, i, u).start()

    def ag_copy(side, c, j):
        e, h = (j // 2, j % 2) if isinstance(j, int) else (lax.div(j, 2), lax.rem(j, 2))
        u = (2 * ahead(-e) + h, 2 * ahead(e) + 1 - h)[side]
        ref = st.at[u, cut(c)]
        return to_z(ref, ref, ag_s.at[side], ag_r.at[side, c, j], (right, left)[side])

    def gather_step(c, j):
        for side in range(2):
            if j >= 2:
                ag_copy(side, c, j - 2).wait_recv()
            if j < 7:
                ag_copy(side, c, j).start()

    def g1(k):
        peer = plane_peer(k)
        return to_row(g_part.at[at(peer, 8)], g_in.at[k], g1_s, g1_r, peer)

    def g2(k):
        piece = g.at[at(row, 8)]
        return to_row(piece, piece, g2_s, g2_r, plane_peer(k))

    def gzc(k):
        return to_z(g_sum, gz.at[z], gz_s, gz_r, lax.rem(z + k, NF))

    def g1_all():
        ref = g_in.at[pl.ds(1, nr - 1)]
        return to_row(ref, ref, g1_s, g1_r, mate)

    def gz_all():
        ref = gz.at[pl.ds(1, NF - 1)]
        return to_z(ref, ref, gz_s, gz_r, right)

    def g2_all():
        ref = g.at[pl.ds(8, 8 * (nr - 1))]
        return to_row(ref, ref, g2_s, g2_r, mate)

    def c1_all(c):
        ref = c_in.at[pl.ds(1, nc - 1), slots[c]]
        return to_row(ref, ref, c1_s.at[c], c1_r.at[c], mate)

    def c2_all(c):
        ref = c_all.at[core, pl.ds(1, nc - 1), slots[c]]
        return to_row(ref, ref, c2_s.at[c], c2_r.at[c], mate)

    def gram_step(stage):
        if stage == 0:
            mine = jnp.concatenate([st[2 * z], st[2 * z + 1]], axis=1)
            g_part[...] = outer(mine, mine, HIGHEST)
            for k in range(1, nr):
                g1(k).start()
        elif stage == 1:
            g1_all().wait_recv()
            total = g_part[at(row, 8), :]
            for k in range(1, nr):
                total = total + g_in[k]
            g_sum[...] = total
            gz[z] = total
            for k in (4, 3, 5, 2, 6, 1, 7):
                gzc(k).start()
        elif stage == 2:
            gz_all().wait_recv()
            total = gz[0]
            for k in range(1, NF):
                total = total + gz[k]
            g[at(row, 8), :] = total
            for k in range(1, nr):
                g2(k).start()
        else:
            g2_all().wait_recv()

    def project(d, c):
        block = ahead(d)
        kc = CHUNKS[c]
        rows = at(block, 2 * hb)
        hi, lo = split(jnp.concatenate([st[2 * block, span[c]], st[2 * block + 1, span[c]]], axis=1))
        both = mm(jnp.concatenate([hi, lo], 0), a_hi[rows, :])
        total = both[:kc] + both[kc:] + mm(hi, a_lo[rows, :])
        c_part[span[c], :] = total if d == 0 else c_part[span[c], :] + total

    def pair(c):
        kh = CHUNKS[c] // 2
        src = c_part.at[pl.ds(pl.multiple_of(starts[c] + (1 - core) * kh, 8), kh)]
        return to_row(src, c_pair.at[pl.ds(starts[c] // 2, kh)], cp_s.at[c], cp_r.at[c], mate)

    def c1(c, k):
        peer = chip_at(steps_to[k - 1])
        return to_row(c_half.at[peer, slots[c]], c_in.at[k, slots[c]], c1_s.at[c], c1_r.at[c], peer * 2 + core)

    def c2(c, k):
        piece = c_all.at[core, chip, slots[c]]
        return to_row(piece, piece, c2_s.at[c], c2_r.at[c], chip_at(steps_to[k - 1]) * 2 + core)

    def back(c):
        ref = c_all.at[core, :, slots[c]]
        return to_row(ref, ref, cf_s.at[c], cf_r.at[c], mate)

    def plane_step(c, stage):
        kh = CHUNKS[c] // 2
        if stage == 0:
            pair(c).start()
        elif stage == 1:
            pair(c).wait_recv()
            mine = pl.ds(pl.multiple_of(starts[c] + core * kh, 8), kh)
            held = c_part[mine, :] + c_pair[starts[c] // 2 : starts[c] // 2 + kh]
            for t in range(kh // 8 * across):
                r, l = divmod(t, across)
                i, s = divmod(t, tiles[c])
                c_half[i, sum(tiles[:c]) + s] = held[8 * r : 8 * r + 8, 128 * l : 128 * l + 128]
            for k in range(1, nc):
                c1(c, k).start()
        elif stage == 2:
            c1_all(c).wait_recv()
            total = c_half[chip, slots[c]]
            for k in range(1, nc):
                total = total + c_in[k, slots[c]]
            c_all[core, chip, slots[c]] = total
            for k in range(1, nc):
                c2(c, k).start()
        else:
            c2_all(c).wait_recv()
            back(c).start()

    def c_copy(c, h):
        piece = (h, slice(None), slots[c])
        return pltpu.make_async_copy(c_all.at[piece], c_out.at[piece], out_sem.at[c])

    def c_land(c):
        back(c).wait_recv()
        for h in range(2):
            c_copy(c, h).start()

    x_copy = pltpu.make_async_copy(ux.at[:, 256:512], x_out, out_sem.at[len(CHUNKS)])
    held_x = []

    def b_copy(i):
        rows = pl.ds(2 * hb * i, 2 * hb)
        return pltpu.make_async_copy(a.at[rows, pl.ds(0, ux.shape[0])], b_out.at[rows], out_sem.at[len(CHUNKS) + 1 + i])

    def turn(d):
        block = ahead(d)
        rows = at(block, 2 * hb)
        s_hi[rows, :], s_lo[rows, :] = split(jnp.concatenate([st[2 * block].T, st[2 * block + 1].T], axis=0))

    def basis_step(i):
        if i == 0:
            x_copy.start()
            held_x.extend(split(ux[:, 256:512]))
        hi, lo = (ref[2 * hb * i : 2 * hb * (i + 1), :] for ref in (s_hi, s_lo))
        block = outer(hi, held_x[0]) + outer(lo, held_x[0]) + outer(hi, held_x[1])
        a[2 * hb * i : 2 * hb * (i + 1), 0 : ux.shape[0]] = block * scale
        b_copy(i).start()

    steps = {
        "N": meet,
        "S": sketch,
        "R": reduce_step,
        "A": gather_step,
        "G": gram_step,
        "P": project,
        "C": plane_step,
        "D": c_land,
        "H": functools.partial(cholesky_step, g=g, ux=ux, win=win, m=m),
        "T": turn,
        "B": basis_step,
    }
    for name, *numbers in PLAN:
        steps[name](*numbers)

    for c in range(len(CHUNKS)):
        pair(c).wait_send()
        back(c).wait_send()
        c1_all(c).wait_send()
        c2_all(c).wait_send()
    for side in range(2):
        ref = rs_buf.at[side]
        to_z(ref, ref, rs_s.at[side], rs_r.at[side, 0, 0], right).wait_send()
        to_z(ref, ref, ag_s.at[side], ag_r.at[side, 0, 0], right).wait_send()
    gz_all().wait_send()
    g1_all().wait_send()
    g2_all().wait_send()
    x_copy.wait()
    for i in range(NF):
        b_copy(i).wait()
    for c in range(len(CHUNKS)):
        for h in range(2):
            c_copy(c, h).wait()


def main(snapshots, test_matrix, nr, scale):
    rows, frames = snapshots.shape
    k = test_matrix.shape[1]
    hb, nc, nq = rows // NF // 2, nr // 2, len(CHUNKS)
    tiles = k * (frames // 128) // 16 // nc
    hbm = pl.BlockSpec(memory_space=pltpu.HBM)
    vm = lambda *shape: pltpu.VMEM(shape, F32)
    vb = lambda *shape: pltpu.VMEM(shape, BF16)
    sem = lambda *shape: pltpu.SemaphoreType.DMA(shape)
    one = pltpu.SemaphoreType.DMA
    return pl.pallas_call(
        functools.partial(main_kernel, nr, scale),
        out_shape=(
            jax.ShapeDtypeStruct((rows, k), F32),
            jax.ShapeDtypeStruct((k, k), F32),
            jax.ShapeDtypeStruct((2, nc, tiles, 8, 128), F32),
        ),
        in_specs=[hbm] * 2,
        out_specs=[hbm] * 3,
        scratch_shapes=[
            vm(rows, frames), vb(rows, frames), vb(rows, frames),
            vm(frames, k), vb(frames, k), vb(frames, k),
            vm(2 * NF, k, hb), vm(2, 7, k, hb), vm(2 * NF, k, hb),
            vm(k, k), vm(nr, 8, k), vm(8, k), vm(NF, 8, k), vm(k, k),
            vm(k, 2 * k), vm(64, k), vm(64, 128),
            vm(k, frames), vm(k // 2, frames), vm(nc, tiles, 8, 128), vm(nc, tiles, 8, 128), vm(2, nc, tiles, 8, 128),
            vb(rows, k), vb(rows, k),
            sem(2, 8), one, sem(2), sem(2, nq, 7), sem(2), sem(2, nq, 7),
            one, one, one, one, one, one,
            sem(nq), sem(nq), sem(nq), sem(nq), sem(nq), sem(nq), sem(nq), sem(nq), sem(nq + 1 + NF),
            pltpu.SemaphoreType.REGULAR((4,)),
        ],
        compiler_params=pltpu.CompilerParams(
            collective_id=0, has_side_effects=True, vmem_limit_bytes=62 * 1024 * 1024
        ),
        name="sketch_gram_projection",
    )(snapshots, test_matrix)


def finish_kernel(b_hbm, x_hbm, c_hbm, basis_hbm, coef_hbm, b, x, c, coef, b_sem, s_sem, in_sem, f_sem):
    parts = b_sem.shape[0]
    per = b_hbm.shape[0] // parts
    loads = [pltpu.make_async_copy(x_hbm, x, in_sem.at[0]), pltpu.make_async_copy(c_hbm, c, in_sem.at[1])]
    passed, stores = [], []
    for i in range(parts):
        rows = pl.ds(i * per, per)
        passed.append(pltpu.make_async_copy(b_hbm.at[rows], b.at[rows], b_sem.at[i]))
        stores.append(pltpu.make_async_copy(b.at[rows], basis_hbm.at[rows], s_sem.at[i]))
    for copy in loads + passed:
        copy.start()
    for load, store in zip(passed, stores):
        load.wait()
        store.start()
    loads[0].wait()
    x_hi, x_lo = split(x[...])
    loads[-1].wait()
    _, nc, total, _, _ = c.shape
    across = coef.shape[1] // 128
    lines = [None] * (x.shape[0] // 8)
    for h in range(2):
        for q, n in enumerate(CHUNKS):
            first, tiles = sum(CHUNKS[:q]) * total // x.shape[0], n * total // x.shape[0]
            for r in range(n // 16):
                line = [divmod(r * across + l, tiles) for l in range(across)]
                place = (sum(CHUNKS[:q]) + h * n // 2) // 8 + r
                lines[place] = jnp.concatenate([c[h, i, first + t] for i, t in line], axis=1)
    c_hi, c_lo = split(jnp.concatenate(lines, axis=0))
    wide = coef.shape[1] // 2
    for i in range(2):
        cols = pl.ds(i * wide, wide)
        hi, lo = (v[:, i * wide : (i + 1) * wide] for v in (c_hi, c_lo))
        coef[:, cols] = mm(x_hi, hi) + mm(x_lo, hi) + mm(x_hi, lo)
        stores.append(pltpu.make_async_copy(coef.at[:, cols], coef_hbm.at[:, cols], f_sem.at[i]))
        stores[-1].start()
    for copy in stores:
        copy.wait()


def finish(b, x, c, frames):
    hbm = pl.BlockSpec(memory_space=pltpu.HBM)
    vm = lambda *shape: pltpu.VMEM(shape, F32)
    return pl.pallas_call(
        finish_kernel,
        out_shape=(jax.ShapeDtypeStruct(b.shape, F32), jax.ShapeDtypeStruct((x.shape[0], frames), F32)),
        in_specs=[hbm] * 3,
        out_specs=[hbm] * 2,
        scratch_shapes=[
            vm(*b.shape), vm(*x.shape), vm(*c.shape), vm(x.shape[0], frames),
            pltpu.SemaphoreType.DMA((4,)), pltpu.SemaphoreType.DMA((4,)), pltpu.SemaphoreType.DMA((2,)), pltpu.SemaphoreType.DMA((2,)),
        ],
        compiler_params=pltpu.CompilerParams(vmem_limit_bytes=62 * 1024 * 1024),
        name="coefficients",
    )(b, x, c)


def on_device(nr, snapshots, test_matrix):
    scale = float((snapshots.shape[0] * nr) ** 0.5)
    b, x, c = main(snapshots, test_matrix, nr, scale)
    return finish(b, x, c, snapshots.shape[1])


def solution(mesh):
    return jax.shard_map(
        functools.partial(on_device, mesh.shape["row"]),
        mesh=mesh,
        in_specs=(P("row", "frame"), P("frame", None)),
        out_specs=(P("row", None), P(None, "frame")),
        check_vma=False,
    )
```

```python
import functools

import jax
import jax.numpy as jnp
from jax import lax
from jax.experimental import pallas as pl
from jax.experimental.pallas import tpu as pltpu
from jax.sharding import PartitionSpec as P

HIGHEST = lax.Precision.HIGHEST
F32 = jnp.float32
BF16 = jnp.bfloat16
MESH = pl.DeviceIdType.MESH
NF = 8
CHUNKS = (96, 96, 64)
CUTS = (96, 96, 64)

PLAN = (
    ("S", 0), ("N", 0), ("R", 0, 0), ("R", 1, 0), ("R", 2, 0), ("S", 1), ("R", 0, 1), ("R", 1, 1), ("R", 2, 1),
    ("S", 2), ("S", 3), ("S", 4), ("R", 0, 2), ("S", 5), ("R", 1, 2), ("S", 6), ("R", 2, 2), ("N", 1), ("S", 7),
    ("R", 0, 3), ("R", 1, 3), ("R", 2, 3), ("N", 2), ("R", 0, 4), ("R", 1, 4), ("R", 2, 4), ("N", 3), ("R", 0, 5),
    ("R", 1, 5), ("R", 2, 5), ("N", 4), ("R", 0, 6), ("R", 1, 6), ("R", 2, 6), ("R", 0, 7), ("R", 1, 7), ("R", 2, 7),
    ("R", 0, 8), ("A", 0, 0), ("A", 0, 1), ("P", 0, 0, 96), ("R", 1, 8), ("A", 1, 0), ("A", 1, 1), ("P", 0, 96, 96),
    ("R", 2, 8), ("G", 0), ("P", 0, 192, 64), ("T", 0), ("A", 0, 2), ("A", 0, 3), ("P", -1, 0, 96), ("P", 1, 0, 96),
    ("A", 1, 2), ("A", 2, 0), ("A", 0, 4), ("A", 0, 5), ("A", 1, 3), ("A", 2, 1), ("G", 1), ("P", -2, 0, 96),
    ("P", 2, 0, 96), ("P", -1, 96, 96), ("P", 1, 96, 96), ("A", 0, 6), ("A", 1, 4), ("A", 2, 2), ("A", 0, 7),
    ("P", -3, 0, 96), ("P", 3, 0, 96), ("A", 1, 5), ("P", -2, 96, 96), ("P", 2, 96, 96), ("A", 2, 3),
    ("P", -1, 192, 64), ("P", 1, 192, 64), ("G", 2), ("T", -1), ("A", 0, 8), ("P", 4, 0, 96), ("C", 0, 0), ("T", 1),
    ("A", 1, 6), ("A", 2, 4), ("C", 0, 1), ("A", 1, 7), ("P", -3, 96, 96), ("P", 3, 96, 96), ("A", 2, 5),
    ("P", -2, 192, 64), ("P", 2, 192, 64), ("T", -2), ("T", 2), ("A", 1, 8), ("P", 4, 96, 96), ("C", 1, 0),
    ("A", 2, 6), ("G", 3), ("H", 0, 0), ("C", 1, 1), ("A", 2, 7), ("P", -3, 192, 64), ("P", 3, 192, 64), ("T", -3),
    ("C", 0, 2), ("A", 2, 8), ("P", 4, 192, 64), ("C", 2, 0), ("T", 3), ("T", 4), ("H", 0, 1), ("C", 2, 1),
    ("H", 1, 0), ("H", 1, 1), ("H", 2, 0), ("C", 1, 2), ("H", 2, 1), ("H", 3, 0), ("C", 0, 3), ("H", 3, 1),
    ("C", 2, 2), ("D", 0), ("B", 0), ("B", 1), ("B", 2), ("B", 3), ("B", 4), ("B", 5), ("B", 6), ("B", 7),
    ("C", 1, 3), ("D", 1), ("C", 2, 3), ("D", 2),
)


def split(x):
    high = x.astype(BF16)
    return high, (x - high.astype(F32)).astype(BF16)


def mm(a, b):
    return jnp.dot(a, b, preferred_element_type=F32)


def inner(a, b):
    return lax.dot_general(a, b, (((0,), (0,)), ((), ())), precision=HIGHEST, preferred_element_type=F32)


def outer(a, b, precision=None):
    return lax.dot_general(a, b, (((1,), (1,)), ((), ())), precision=precision, preferred_element_type=F32)


def at(i, size):
    return pl.ds(pl.multiple_of(i * size, size), size)


def iota(shape, dim):
    return lax.broadcasted_iota(jnp.int32, shape, dim)


def panel_begin(p, g, ux, win, m):
    lo, hi = 64 * p, 64 * p + 64
    rows = g[lo:hi, :]
    if p:
        rows = jnp.concatenate([rows[:, lo:], jnp.zeros((64, lo), F32)], axis=1)
        rows = rows - inner(ux[0:lo, lo:hi], ux[0:lo, lo : lo + 256])
    win[...] = rows
    eye = jnp.where(iota((64, 64), 0) == iota((64, 64), 1), 1.0, 0.0)
    m[...] = jnp.concatenate([rows[:, 0:64], eye], axis=1)


def eliminate(m, groups):
    sub = iota((8, 128), 0)
    lanes = lambda x, k: jnp.broadcast_to(x[:, k : k + 1], (8, 128))
    subl = lambda x, k: jnp.broadcast_to(x[k : k + 1, :], (8, 128))
    tiles = {i: m[8 * i : 8 * i + 8, :] for i in range(groups[0], 8)}
    own = [lanes(tiles[groups[0]], 8 * groups[0] + k) for k in range(8)]
    for t in groups:
        cols = {i: [lanes(tiles[i], 8 * t + k) for k in range(8)] for i in range(t + 1, 8)}
        cols[t] = own
        more = t + 1 in groups
        if more:
            own = [lanes(tiles[t + 1], 8 * t + 8 + k) for k in range(8)]
        pivots = jnp.ones((8, 128), F32)
        for k in range(8):
            row = subl(tiles[t], k)
            pivot = subl(cols[t][k], k)
            inv = 1.0 / pivot
            pivots = jnp.where(sub == k, pivot, pivots)
            ahead = {j: subl(cols[t][j], k) for j in range(k + 1, 8)}
            for i in range(t, 8):
                mult = cols[i][k] * inv
                if i == t:
                    mult = jnp.where(sub > k, mult, 0.0)
                if more and i == t + 1:
                    own = [own[j] - mult * subl(cols[i][k], j) for j in range(8)]
                tiles[i] = tiles[i] - mult * row
                for j in range(k + 1, 8):
                    cols[i][j] = cols[i][j] - mult * ahead[j]
        m[8 * t : 8 * t + 8, :] = tiles[t] / jnp.sqrt(pivots)
    for i in range(groups[-1] + 1, 8):
        m[8 * i : 8 * i + 8, :] = tiles[i]


def panel_end(p, ux, win, m):
    lo, hi = 64 * p, 64 * p + 64
    w = jnp.where(iota((64, 64), 1) <= iota((64, 64), 0), m[:, 64:128], 0.0)
    ux[lo:hi, lo : lo + 256] = jnp.dot(w, win[...], precision=HIGHEST, preferred_element_type=F32)
    ux[lo:hi, 256 + lo : 256 + hi] = w


def cholesky_step(p, half, g, ux, win, m):
    if half == 0:
        panel_begin(p, g, ux, win, m)
    eliminate(m, range(4 * half, 4 * half + 4))
    if half == 1:
        panel_end(p, ux, win, m)


def main_kernel(nr, scale, *refs):
    a_hbm, w_hbm, b_out, x_out, c_out = refs[:5]
    a, a_hi, a_lo, w, w_hi, w_lo, part, rs_buf, st = refs[5:14]
    g_part, g_in, g_sum, gz, g, ux, win, m = refs[14:22]
    c_part, c_pair, c_half, c_in, c_all, s_hi, s_lo = refs[22:29]
    a_sem, w_sem, rs_s, rs_r, ag_s, ag_r, g1_s, g1_r, gz_s, gz_r, g2_s, g2_r = refs[29:41]
    cp_s, cp_r, c1_s, c1_r, c2_s, c2_r, cf_s, cf_r, out_sem, near = refs[41:]
    row, z = lax.axis_index("row"), lax.axis_index("frame")
    right, left = lax.rem(z + 1, NF), lax.rem(z + NF - 1, NF)
    core, chip = lax.rem(row, 2), lax.div(row, 2)
    mate = row + 1 - 2 * core
    nc = nr // 2
    hb = st.shape[2]
    frames = a.shape[1]
    across = frames // 128
    ahead = lambda d: lax.rem(z + d + NF, NF)
    rows_of = lambda u: at(u, hb)
    starts = [sum(CHUNKS[:c]) for c in range(len(CHUNKS))]
    span = [slice(starts[c], starts[c] + CHUNKS[c]) for c in range(len(CHUNKS))]
    cut = lambda c: pl.ds(starts[c], CHUNKS[c])
    firsts = [sum(CUTS[:c]) for c in range(len(CUTS))]
    tiles = [n * across // 16 // nc for n in CUTS]
    slots = [pl.ds(sum(tiles[:c]), tiles[c]) for c in range(len(CUTS))]

    def to_z(src, dst, s, r, peer):
        return pltpu.make_async_remote_copy(src, dst, s, r, device_id={"frame": peer}, device_id_type=MESH)

    def to_row(src, dst, s, r, peer):
        return pltpu.make_async_remote_copy(src, dst, s, r, device_id={"row": peer}, device_id_type=MESH)

    def loop(first, last, f):
        def body(k, carry):
            f(k)
            return carry

        lax.fori_loop(first, last, body, 0)

    barrier = pltpu.get_barrier_semaphore()
    nx = 4
    x, y, ny = lax.rem(chip, nx), lax.div(chip, nx), nc // nx
    at_chip = lambda yy, xx: {"row": (lax.rem(yy + ny, ny) * nx + lax.rem(xx + nx, nx)) * 2 + core}
    neighbours = ({"frame": right}, {"frame": left}, {"row": mate})
    neighbours += (at_chip(y, x + 1), at_chip(y, x - 1), at_chip(y + 1, x), at_chip(y - 1, x))

    far = lambda o: min(o[0], ny - o[0]) + min(o[1], nx - o[1])
    steps_to = sorted(((dy, dx) for dy in range(ny) for dx in range(nx)), key=lambda o: (-far(o), o))
    chip_at = lambda o: lax.rem(y + o[0], ny) * nx + lax.rem(x + o[1], nx)
    both_cores = [(o, flip) for o in steps_to for flip in (0, 1)][:-2] + [((0, 0), 1)]

    def plane_peer(k):
        o, flip = both_cores[k - 1]
        return 2 * chip_at(o) + (1 - core if flip else core)

    def greet(which):
        for peer in neighbours:
            pl.semaphore_signal(which, inc=1, device_id=peer, device_id_type=MESH)

    def greeted(which):
        pl.semaphore_wait(which, len(neighbours))

    def meet(stage):
        if stage:
            greeted(near.at[stage - 1])
        else:
            greeted(barrier)
        if stage < 4:
            greet(near.at[stage])

    greet(barrier)

    def units(i):
        if isinstance(i, int):
            d, h = ((8 - i) // 2, i % 2) if i < 8 else (0, 0)
        else:
            d, h = lax.div(8 - i, 2), lax.rem(i, 2)
        return 2 * ahead(d) + h, 2 * ahead(-d) + 1 - h

    def load(u, side, i):
        return pltpu.make_async_copy(a_hbm.at[rows_of(u)], a.at[rows_of(u)], a_sem.at[side, i])

    w_copy = pltpu.make_async_copy(w_hbm, w, w_sem)

    def fetch(i):
        for side, u in enumerate(units(i)):
            load(u, side, i).start()

    w_copy.start()
    fetch(0)
    fetch(1)
    ux[:, 256:512] = jnp.zeros((ux.shape[0], 256), F32)
    w_copy.wait()
    fetch(2)
    w_hi[...], w_lo[...] = split(w[...])

    def sketch(i):
        if i + 3 < 8:
            fetch(i + 3)
        both = units(i)
        for side, u in enumerate(both):
            load(u, side, i).wait()
        hi, lo = split(jnp.concatenate([a[rows_of(u), :] for u in both], axis=0))
        for side, u in enumerate(both):
            held = slice(side * hb, (side + 1) * hb)
            a_hi[rows_of(u), :], a_lo[rows_of(u), :] = hi[held], lo[held]
        halves = mm(jnp.concatenate([hi, lo], axis=0), w_hi[...])
        total = halves[: 2 * hb] + halves[2 * hb :] + mm(hi, w_lo[...])
        for side, u in enumerate(both):
            part[u] = total[side * hb : (side + 1) * hb].T

    def rs_copy(side, c, i, u):
        dst = rs_buf.at[side, i, cut(c)]
        return to_z(part.at[u, cut(c)], dst, rs_s.at[side], rs_r.at[side, c, i], (right, left)[side])

    def reduce_step(c, i):
        for side, u in enumerate(units(i)):
            if i >= 2:
                rs_copy(side, c, i - 2, u).wait_recv()
                total = part[u, span[c]] + rs_buf[side, i - 2, span[c]]
                if i < 8:
                    part[u, span[c]] = total
                else:
                    st[u, span[c]] = total
            if i < 7:
                rs_copy(side, c, i, u).start()

    def ag_copy(side, c, j):
        e, h = (j // 2, j % 2) if isinstance(j, int) else (lax.div(j, 2), lax.rem(j, 2))
        u = (2 * ahead(-e) + h, 2 * ahead(e) + 1 - h)[side]
        ref = st.at[u, cut(c)]
        return to_z(ref, ref, ag_s.at[side], ag_r.at[side, c, j], (right, left)[side])

    def gather_step(c, j):
        for side in range(2):
            if j >= 2:
                ag_copy(side, c, j - 2).wait_recv()
            if j < 7:
                ag_copy(side, c, j).start()

    def g1(k):
        peer = plane_peer(k)
        return to_row(g_part.at[at(peer, 8)], g_in.at[k], g1_s, g1_r, peer)

    def g2(k):
        piece = g.at[at(row, 8)]
        return to_row(piece, piece, g2_s, g2_r, plane_peer(k))

    def gzc(k):
        return to_z(g_sum, gz.at[z], gz_s, gz_r, lax.rem(z + k, NF))

    def g1_all():
        ref = g_in.at[pl.ds(1, nr - 1)]
        return to_row(ref, ref, g1_s, g1_r, mate)

    def gz_all():
        ref = gz.at[pl.ds(1, NF - 1)]
        return to_z(ref, ref, gz_s, gz_r, right)

    def g2_all():
        ref = g.at[pl.ds(8, 8 * (nr - 1))]
        return to_row(ref, ref, g2_s, g2_r, mate)

    def c1_all(c):
        ref = c_in.at[pl.ds(1, nc - 1), slots[c]]
        return to_row(ref, ref, c1_s.at[c], c1_r.at[c], mate)

    def c2_all(c):
        ref = c_all.at[core, pl.ds(1, nc - 1), slots[c]]
        return to_row(ref, ref, c2_s.at[c], c2_r.at[c], mate)

    def gram_step(stage):
        if stage == 0:
            mine = jnp.concatenate([st[2 * z], st[2 * z + 1]], axis=1)
            g_part[...] = outer(mine, mine, HIGHEST)
            for k in range(1, nr):
                g1(k).start()
        elif stage == 1:
            g1_all().wait_recv()
            total = g_part[at(row, 8), :]
            for k in range(1, nr):
                total = total + g_in[k]
            g_sum[...] = total
            gz[z] = total
            for k in (4, 3, 5, 2, 6, 1, 7):
                gzc(k).start()
        elif stage == 2:
            gz_all().wait_recv()
            total = gz[0]
            for k in range(1, NF):
                total = total + gz[k]
            g[at(row, 8), :] = total
            for k in range(1, nr):
                g2(k).start()
        else:
            g2_all().wait_recv()

    def project(d, first, n):
        block = ahead(d)
        cols = slice(first, first + n)
        rows = at(block, 2 * hb)
        hi, lo = split(jnp.concatenate([st[2 * block, cols], st[2 * block + 1, cols]], axis=1))
        both = mm(jnp.concatenate([hi, lo], 0), a_hi[rows, :])
        total = both[:n] + both[n:] + mm(hi, a_lo[rows, :])
        c_part[cols, :] = total if d == 0 else c_part[cols, :] + total

    def pair(c):
        kh = CUTS[c] // 2
        src = c_part.at[pl.ds(pl.multiple_of(firsts[c] + (1 - core) * kh, 8), kh)]
        return to_row(src, c_pair.at[pl.ds(firsts[c] // 2, kh)], cp_s.at[c], cp_r.at[c], mate)

    def c1(c, k):
        peer = chip_at(steps_to[k - 1])
        return to_row(c_half.at[peer, slots[c]], c_in.at[k, slots[c]], c1_s.at[c], c1_r.at[c], peer * 2 + core)

    def c2(c, k):
        piece = c_all.at[core, chip, slots[c]]
        return to_row(piece, piece, c2_s.at[c], c2_r.at[c], chip_at(steps_to[k - 1]) * 2 + core)

    def back(c):
        ref = c_all.at[core, :, slots[c]]
        return to_row(ref, ref, cf_s.at[c], cf_r.at[c], mate)

    def plane_step(c, stage):
        kh = CUTS[c] // 2
        if stage == 0:
            pair(c).start()
        elif stage == 1:
            pair(c).wait_recv()
            mine = pl.ds(pl.multiple_of(firsts[c] + core * kh, 8), kh)
            held = c_part[mine, :] + c_pair[firsts[c] // 2 : firsts[c] // 2 + kh]
            for t in range(kh // 8 * across):
                r, l = divmod(t, across)
                i, s = divmod(t, tiles[c])
                c_half[i, sum(tiles[:c]) + s] = held[8 * r : 8 * r + 8, 128 * l : 128 * l + 128]
            for k in range(1, nc):
                c1(c, k).start()
        elif stage == 2:
            c1_all(c).wait_recv()
            total = c_half[chip, slots[c]]
            for k in range(1, nc):
                total = total + c_in[k, slots[c]]
            c_all[core, chip, slots[c]] = total
            for k in range(1, nc):
                c2(c, k).start()
        else:
            c2_all(c).wait_recv()
            back(c).start()

    def c_copy(c, h):
        piece = (h, slice(None), slots[c])
        return pltpu.make_async_copy(c_all.at[piece], c_out.at[piece], out_sem.at[c])

    def c_land(c):
        back(c).wait_recv()
        for h in range(2):
            c_copy(c, h).start()

    x_copy = pltpu.make_async_copy(ux.at[:, 256:512], x_out, out_sem.at[len(CUTS)])
    held_x = []

    def b_copy(i):
        rows = pl.ds(2 * hb * i, 2 * hb)
        return pltpu.make_async_copy(a.at[rows, pl.ds(0, ux.shape[0])], b_out.at[rows], out_sem.at[len(CUTS) + 1 + i])

    def turn(d):
        block = ahead(d)
        rows = at(block, 2 * hb)
        s_hi[rows, :], s_lo[rows, :] = split(jnp.concatenate([st[2 * block].T, st[2 * block + 1].T], axis=0))

    def basis_step(i):
        if i == 0:
            x_copy.start()
            held_x.extend(split(ux[:, 256:512]))
        hi, lo = (ref[2 * hb * i : 2 * hb * (i + 1), :] for ref in (s_hi, s_lo))
        block = outer(hi, held_x[0]) + outer(lo, held_x[0]) + outer(hi, held_x[1])
        a[2 * hb * i : 2 * hb * (i + 1), 0 : ux.shape[0]] = block * scale
        b_copy(i).start()

    steps = {
        "N": meet,
        "S": sketch,
        "R": reduce_step,
        "A": gather_step,
        "G": gram_step,
        "P": project,
        "C": plane_step,
        "D": c_land,
        "H": functools.partial(cholesky_step, g=g, ux=ux, win=win, m=m),
        "T": turn,
        "B": basis_step,
    }
    for name, *numbers in PLAN:
        steps[name](*numbers)

    for c in range(len(CUTS)):
        pair(c).wait_send()
        back(c).wait_send()
        c1_all(c).wait_send()
        c2_all(c).wait_send()
    for side in range(2):
        ref = rs_buf.at[side]
        to_z(ref, ref, rs_s.at[side], rs_r.at[side, 0, 0], right).wait_send()
        to_z(ref, ref, ag_s.at[side], ag_r.at[side, 0, 0], right).wait_send()
    gz_all().wait_send()
    g1_all().wait_send()
    g2_all().wait_send()
    x_copy.wait()
    for i in range(NF):
        b_copy(i).wait()
    for c in range(len(CUTS)):
        for h in range(2):
            c_copy(c, h).wait()


def main(snapshots, test_matrix, nr, scale):
    rows, frames = snapshots.shape
    k = test_matrix.shape[1]
    hb, nc, nq, ncut = rows // NF // 2, nr // 2, len(CHUNKS), len(CUTS)
    tiles = k * (frames // 128) // 16 // nc
    hbm = pl.BlockSpec(memory_space=pltpu.HBM)
    vm = lambda *shape: pltpu.VMEM(shape, F32)
    vb = lambda *shape: pltpu.VMEM(shape, BF16)
    sem = lambda *shape: pltpu.SemaphoreType.DMA(shape)
    one = pltpu.SemaphoreType.DMA
    return pl.pallas_call(
        functools.partial(main_kernel, nr, scale),
        out_shape=(
            jax.ShapeDtypeStruct((rows, k), F32),
            jax.ShapeDtypeStruct((k, k), F32),
            jax.ShapeDtypeStruct((2, nc, tiles, 8, 128), F32),
        ),
        in_specs=[hbm] * 2,
        out_specs=[hbm] * 3,
        scratch_shapes=[
            vm(rows, frames), vb(rows, frames), vb(rows, frames),
            vm(frames, k), vb(frames, k), vb(frames, k),
            vm(2 * NF, k, hb), vm(2, 7, k, hb), vm(2 * NF, k, hb),
            vm(k, k), vm(nr, 8, k), vm(8, k), vm(NF, 8, k), vm(k, k),
            vm(k, 2 * k), vm(64, k), vm(64, 128),
            vm(k, frames), vm(k // 2, frames), vm(nc, tiles, 8, 128), vm(nc, tiles, 8, 128), vm(2, nc, tiles, 8, 128),
            vb(rows, k), vb(rows, k),
            sem(2, 8), one, sem(2), sem(2, nq, 7), sem(2), sem(2, nq, 7),
            one, one, one, one, one, one,
            sem(ncut), sem(ncut), sem(ncut), sem(ncut), sem(ncut), sem(ncut), sem(ncut), sem(ncut), sem(ncut + 1 + NF),
            pltpu.SemaphoreType.REGULAR((4,)),
        ],
        compiler_params=pltpu.CompilerParams(
            collective_id=0, has_side_effects=True, vmem_limit_bytes=62 * 1024 * 1024
        ),
        name="sketch_gram_projection",
    )(snapshots, test_matrix)


def finish_kernel(b_hbm, x_hbm, c_hbm, basis_hbm, coef_hbm, b, x, c, coef, b_sem, s_sem, in_sem, f_sem):
    parts = b_sem.shape[0]
    per = b_hbm.shape[0] // parts
    loads = [pltpu.make_async_copy(x_hbm, x, in_sem.at[0]), pltpu.make_async_copy(c_hbm, c, in_sem.at[1])]
    passed, stores = [], []
    for i in range(parts):
        rows = pl.ds(i * per, per)
        passed.append(pltpu.make_async_copy(b_hbm.at[rows], b.at[rows], b_sem.at[i]))
        stores.append(pltpu.make_async_copy(b.at[rows], basis_hbm.at[rows], s_sem.at[i]))
    for copy in loads + passed:
        copy.start()
    for load, store in zip(passed, stores):
        load.wait()
        store.start()
    loads[0].wait()
    x_hi, x_lo = split(x[...])
    loads[-1].wait()
    _, nc, total, _, _ = c.shape
    across = coef.shape[1] // 128
    lines = [None] * (x.shape[0] // 8)
    for h in range(2):
        for q, n in enumerate(CUTS):
            first, tiles = sum(CUTS[:q]) * total // x.shape[0], n * total // x.shape[0]
            for r in range(n // 16):
                line = [divmod(r * across + l, tiles) for l in range(across)]
                place = (sum(CUTS[:q]) + h * n // 2) // 8 + r
                lines[place] = jnp.concatenate([c[h, i, first + t] for i, t in line], axis=1)
    c_hi, c_lo = split(jnp.concatenate(lines, axis=0))
    wide = coef.shape[1] // 2
    for i in range(2):
        cols = pl.ds(i * wide, wide)
        hi, lo = (v[:, i * wide : (i + 1) * wide] for v in (c_hi, c_lo))
        coef[:, cols] = mm(x_hi, hi) + mm(x_lo, hi) + mm(x_hi, lo)
        stores.append(pltpu.make_async_copy(coef.at[:, cols], coef_hbm.at[:, cols], f_sem.at[i]))
        stores[-1].start()
    for copy in stores:
        copy.wait()


def finish(b, x, c, frames):
    hbm = pl.BlockSpec(memory_space=pltpu.HBM)
    vm = lambda *shape: pltpu.VMEM(shape, F32)
    return pl.pallas_call(
        finish_kernel,
        out_shape=(jax.ShapeDtypeStruct(b.shape, F32), jax.ShapeDtypeStruct((x.shape[0], frames), F32)),
        in_specs=[hbm] * 3,
        out_specs=[hbm] * 2,
        scratch_shapes=[
            vm(*b.shape), vm(*x.shape), vm(*c.shape), vm(x.shape[0], frames),
            pltpu.SemaphoreType.DMA((4,)), pltpu.SemaphoreType.DMA((4,)), pltpu.SemaphoreType.DMA((2,)), pltpu.SemaphoreType.DMA((2,)),
        ],
        compiler_params=pltpu.CompilerParams(vmem_limit_bytes=62 * 1024 * 1024),
        name="coefficients",
    )(b, x, c)


def on_device(nr, snapshots, test_matrix):
    scale = float((snapshots.shape[0] * nr) ** 0.5)
    b, x, c = main(snapshots, test_matrix, nr, scale)
    return finish(b, x, c, snapshots.shape[1])


def solution(mesh):
    return jax.shard_map(
        functools.partial(on_device, mesh.shape["row"]),
        mesh=mesh,
        in_specs=(P("row", "frame"), P("frame", None)),
        out_specs=(P("row", None), P(None, "frame")),
        check_vma=False,
    )
```
